32 devices in a mesh: dp: 8 (over z, core), seq: 4 (over y, x).
Axes of the slice: x: 2, y: 2, z: 4, core: 2. Of those that a mesh axis runs over, the one named last changes fastest.
Arguments:
- tokens: bfloat16 [4096, 1280], P(('dp', 'seq')), parts along dimension 0, may hold values from -6 to 6
- segment_ids: int32 [4096], P('dp'), parts along dimension 0, may hold values from 0 to 7, as said below
- w_qkv: bfloat16 [1280, 3840], P(None, 'seq')
- w_out: bfloat16 [1280, 1280], P('seq'), may hold values from -0.15625 to 0.15625
- w_merge: bfloat16 [5120, 4096], P(None, 'seq'), may hold values from -0.078125 to 0.078125
- gain_attn: float32 [1280], replicated, may hold values from 0.1 to 1.9
- gain_merge: float32 [1280], replicated, may hold values from 0.1 to 1.9
Outputs:
- merged_out: bfloat16 [1024, 4096], P(('dp', 'seq')), parts along dimension 0
The draws below stay inside these ranges and needn't reach their ends.
There are 8 independent parts, one for each index of `dp`. The reference program is written for one: setup_inputs(seed, part) draws one part's arguments, and reference() takes and returns one part's arrays. A program takes and returns all parts, laid end to end along the dimension named above; an argument that names none is the same for every part. Nothing has to cross between parts.
Inputs may be any that keep to these rules, and one draw needn't show every extreme that they name: `segment_ids`: Non-decreasing along the packed tokens, starting at 0, rising by 0 or 1 from one token to the next, and equal within every aligned group of 4 tokens (an image's 2x2 patch blocks are stored together). There are exactly 8 images.
All inputs are finite; a program needn't handle non-finite values.
Results may differ from the reference program's by a relative error of at most 0.011.
Values may be sent and summed in bfloat16 or wider, within the bound.
A program may use at most 64 MiB of HBM per device.

```python
import jax
import jax.numpy as jnp
from jax import lax

D = 1280
HEADS = 16
HEAD_DIM = 80
OUT = 4096
TOK_DEV = 128
TOKENS = 512
MERGED = 128


def packed_layout(key):
    block_count = TOKENS // 4
    image_count = 2 * (TOKENS // TOK_DEV)
    window = block_count // 2
    window_start = jax.random.randint(jax.random.fold_in(key, 1), (), 0, block_count - window + 1).astype(jnp.int32)
    position = jnp.arange(block_count, dtype=jnp.int32)
    ranks = jax.random.permutation(jax.random.fold_in(key, 2), block_count).astype(jnp.int32)
    barred = (position == 0) | (position > window_start) & (position < window_start + window)
    scored = ranks + barred.astype(jnp.int32) * block_count
    chosen = jnp.argsort(scored)[:image_count - 1]
    starts = jnp.zeros((block_count,), jnp.int32).at[chosen].set(1)
    image_ids = jnp.cumsum(starts).astype(jnp.int32)
    return (jnp.repeat(image_ids, 4).astype(jnp.int32), window_start, window)


def draw_segment_ids(key, part):
    layout = packed_layout(jax.random.fold_in(key, 11))
    return layout[0]


def draw_tokens(key, part):
    layout = packed_layout(jax.random.fold_in(key, 11))
    window_start = layout[1]
    window = layout[2]
    half_window = window // 2
    block_of = jnp.arange(TOKENS, dtype=jnp.int32) // 4
    first_half = (block_of >= window_start) & (block_of < window_start + half_window)
    second_half = (block_of >= window_start + half_window) & (block_of < window_start + window)
    sign_field = first_half.astype(jnp.float32) - second_half.astype(jnp.float32)
    direction = jax.random.uniform(jax.random.fold_in(key, 12), (D,), jnp.float32, -1.0, 1.0)
    base = jnp.clip(jax.random.normal(jax.random.fold_in(key, 13), (TOKENS, D), jnp.float32), -4.0, 4.0)
    shifted = base + 2.0 * sign_field[:, None] * direction[None, :]
    return shifted.astype(jnp.bfloat16)


def draw_w_qkv(key, part):
    base = jax.random.normal(key, (D, HEADS, 3, HEAD_DIM), jnp.float32) * D ** (-0.5)
    return base.reshape(D, 3 * D).astype(jnp.bfloat16)


def block_scale(key, extent, cuts, low, largest):
    def one(axis_at, parts):
        heights = jax.random.uniform(jax.random.fold_in(jax.random.fold_in(key, 6), axis_at), (parts,), jnp.float32, low / len(cuts), largest / len(cuts))
        return jnp.repeat(jnp.exp(heights), extent[axis_at] // parts).reshape((-1,) + (1,) * (len(extent) - axis_at - 1))

    level = one(*cuts[0])
    for cut in cuts[1:]:
        level = level * one(*cut)
    return level


def scatter_about(key, dims, spread, limit, pieces=(), kind=jnp.bfloat16):
    gain = block_scale(key, dims, pieces, -0.22, 0.18) if pieces else 1.0
    array = jax.random.normal(key, dims, jnp.float32) * spread * gain
    return jnp.minimum(jnp.maximum(array, -limit), limit).astype(kind)


def setup_inputs(seed: int = 0, part: int = 0) -> dict:
    arg_keys = jax.random.split(jax.random.key(seed), 8)
    own_keys = jax.random.split(jax.random.fold_in(arg_keys[7], part), 8)
    return {
        "tokens": draw_tokens(jax.random.fold_in(jax.random.fold_in(arg_keys[7], part), 71), part),
        "segment_ids": draw_segment_ids(jax.random.fold_in(jax.random.fold_in(arg_keys[7], part), 71), part),
        "w_qkv": draw_w_qkv(jax.random.fold_in(arg_keys[7], 71), part),
        "w_out": scatter_about(arg_keys[3], (D, D), D ** -0.5, 0.15625, ((0, 4),)),
        "w_merge": scatter_about(arg_keys[4], (4 * D, OUT), (4 * D) ** -0.5, 0.078125, ((1, 4),)),
        "gain_attn": jnp.clip(1.0 + 0.18 * jax.random.normal(arg_keys[5], (D,), jnp.float32), 0.1, 1.9),
        "gain_merge": jnp.clip(1.0 + 0.18 * jax.random.normal(arg_keys[6], (D,), jnp.float32), 0.1, 1.9),
    }


def layer_norm(vector, scale_gain):
    average = lax.optimization_barrier(jnp.mean(vector, axis=-1, keepdims=True))
    centred = vector - average
    spread_sq = lax.optimization_barrier(jnp.mean(centred * centred, axis=-1, keepdims=True))
    return centred * lax.rsqrt(spread_sq + 1e-06) * scale_gain.astype(jnp.float32)

def reference(tokens, segment_ids, w_qkv, w_out, w_merge, gain_attn, gain_merge):
    residual = tokens.astype(jnp.float32)
    normed = layer_norm(residual, gain_attn).astype(jnp.bfloat16)
    qkv = jnp.dot(normed, w_qkv, preferred_element_type=jnp.float32).astype(jnp.bfloat16)
    per_head = jnp.moveaxis(qkv.reshape(TOKENS, HEADS, 3, HEAD_DIM), 1, 0)
    same_image = segment_ids[:, None] == segment_ids[None, :]

    def one_head(head_block):
        queries = head_block[:, 0, :]
        key_rows = head_block[:, 1, :]
        value_rows = head_block[:, 2, :]
        scores = jnp.dot(queries, key_rows.T, preferred_element_type=jnp.float32) * HEAD_DIM ** (-0.5)
        scores = jnp.where(same_image, scores, -jnp.inf)
        row_max = lax.optimization_barrier(jnp.max(scores, axis=-1, keepdims=True))
        expo = jnp.where(same_image, jnp.exp(scores - row_max), 0.0)
        row_sum = lax.optimization_barrier(jnp.sum(expo, axis=-1, keepdims=True))
        probs = expo.astype(jnp.bfloat16)
        result = jnp.dot(probs, value_rows, preferred_element_type=jnp.float32) / row_sum
        return result.astype(jnp.bfloat16)
    heads_out = lax.map(one_head, per_head)
    attended = jnp.moveaxis(heads_out, 0, 1).reshape(TOKENS, D)
    hidden = residual + jnp.dot(attended, w_out, preferred_element_type=jnp.float32)
    normed_two = layer_norm(hidden, gain_merge).astype(jnp.bfloat16)
    merged = normed_two.reshape(MERGED, 4 * D)
    return jnp.dot(merged, w_merge, preferred_element_type=jnp.float32).astype(jnp.bfloat16)
```

```python
import functools

import jax
import jax.numpy as jnp
from jax import lax
from jax.experimental import pallas as pl
from jax.experimental.pallas import tpu as pltpu
from jax.sharding import PartitionSpec as P

HEADS = 16
HEAD_DIM = 80
LOG2E = 1.4426950408889634
MESH = pl.DeviceIdType.MESH


def layer_norm(vector, scale_gain):
    average = jnp.mean(vector, axis=-1, keepdims=True)
    centred = vector - average
    spread_sq = jnp.mean(centred * centred, axis=-1, keepdims=True)
    return centred * lax.rsqrt(spread_sq + 1e-06) * scale_gain


def block_kernel(
    n, tok_ref, ids_ref, wqkv_hbm, wout_hbm, wmerge_hbm, ga_ref, gm_ref, out_ref,
    wqkv, wout, wmerge, nslots, qs, ks, vs, kid, att, psend, pslots, own, flat, mslots, obuf,
    local_sem, a_send, a_recv, p_send, p_recv, m_send, m_recv, o_send, o_recv,
):
    me = lax.axis_index("seq")
    dp = lax.axis_index("dp")
    rows = tok_ref.shape[0]
    width = tok_ref.shape[1]
    heads = qs.shape[0]
    bits = n.bit_length() - 1
    quarter = rows // 4
    cols = wmerge_hbm.shape[1]

    def peer(d):
        total = 0
        for b in range(bits):
            total = total + (((me // (1 << b)) + (d // (1 << b))) % 2) * (1 << b)
        return total

    def remote(src, dst, send, recv, d):
        return pltpu.make_async_remote_copy(
            src_ref=src, dst_ref=dst, send_sem=send, recv_sem=recv,
            device_id=(dp, peer(d)), device_id_type=MESH,
        )

    def copy_a(d):
        return remote(nslots.at[0], nslots.at[d], a_send.at[d], a_recv.at[d], d)

    def copy_p(d):
        return remote(psend.at[d], pslots.at[d], p_send.at[d], p_recv.at[d], d)

    def copy_m(j, d):
        return remote(
            mslots.at[j, pl.ds(0, quarter)],
            mslots.at[j, pl.ds(d * quarter, quarter)],
            m_send.at[j, d], m_recv.at[j, d], d,
        )

    def copy_o(d):
        return remote(
            obuf.at[pl.ds(d * quarter, quarter)],
            out_ref.at[:, pl.ds(pl.multiple_of(me * cols, 128), cols)],
            o_send.at[d], o_recv.at[d], d,
        )

    barrier = pltpu.get_barrier_semaphore()
    for d in range(1, n):
        pl.semaphore_signal(barrier, inc=1, device_id=(dp, peer(d)), device_id_type=MESH)
    load_qkv = pltpu.make_async_copy(wqkv_hbm, wqkv, local_sem.at[0])
    load_out = pltpu.make_async_copy(wout_hbm, wout, local_sem.at[1])
    load_merge = pltpu.make_async_copy(wmerge_hbm, wmerge, local_sem.at[2])
    load_qkv.start()
    load_out.start()
    load_merge.start()

    nslots[0] = layer_norm(tok_ref[...].astype(jnp.float32), ga_ref[...]).astype(jnp.bfloat16)
    pl.semaphore_wait(barrier, n - 1)
    for d in range(n - 1, 0, -1):
        copy_a(d).start()

    for d in range(n):
        kid[0:1, d * rows:(d + 1) * rows] = ids_ref[pl.ds(peer(d), 1), :].astype(jnp.float32)

    load_qkv.wait()
    load_out.wait()

    def qkv_step(d, carry):
        @pl.when(d > 0)
        def _():
            copy_a(d).wait_recv()

        prod = jnp.dot(nslots[d], wqkv[...], preferred_element_type=jnp.float32)
        prod = prod.astype(jnp.bfloat16)
        at = pl.ds(pl.multiple_of(d * rows, rows), rows)
        for h in range(heads):
            base = 3 * HEAD_DIM * h
            qs[h, at, :] = prod[:, base:base + HEAD_DIM]
            ks[h, at, :] = prod[:, base + HEAD_DIM:base + 2 * HEAD_DIM]
            vs[h, at, :] = prod[:, base + 2 * HEAD_DIM:base + 3 * HEAD_DIM]
        return carry

    lax.fori_loop(0, n, qkv_step, 0)

    factor = HEAD_DIM ** (-0.5) * LOG2E

    def attend_step(i, carry):
        d = n - 1 - i
        id_row = ids_ref[pl.ds(peer(d), 1), :].astype(jnp.float32)
        query_ids = jnp.broadcast_to(id_row, (rows, rows)).T[:, 0:1]
        same_image = query_ids == kid[...]
        at = pl.ds(pl.multiple_of(d * rows, rows), rows)
        for h in range(heads):
            scores = lax.dot_general(
                qs[h, at, :], ks[h], (((1,), (1,)), ((), ())),
                preferred_element_type=jnp.float32,
            )
            scores = jnp.where(same_image, scores * factor, -jnp.inf)
            expo = jnp.exp2(scores - jnp.max(scores, axis=-1, keepdims=True))
            row_sum = jnp.sum(expo, axis=-1, keepdims=True)
            summed = jnp.dot(
                expo.astype(jnp.bfloat16), vs[h], preferred_element_type=jnp.float32
            )
            att[:, h * HEAD_DIM:(h + 1) * HEAD_DIM] = (summed / row_sum).astype(jnp.bfloat16)
        part = jnp.dot(att[...], wout[...], preferred_element_type=jnp.float32)

        @pl.when(d > 0)
        def _():
            psend[d] = part.astype(jnp.bfloat16)
            copy_p(d).start()

        @pl.when(d == 0)
        def _():
            own[...] = part

        return carry

    lax.fori_loop(0, n, attend_step, 0)

    hidden = own[...] + tok_ref[...].astype(jnp.float32)
    for d in range(n - 1, 0, -1):
        copy_p(d).wait_recv()
        hidden = hidden + pslots[d].astype(jnp.float32)
    normed_two = layer_norm(hidden, gm_ref[...])
    lanes = flat.shape[2]
    for c in range(width // lanes):
        flat[c] = normed_two[:, c * lanes:(c + 1) * lanes]
    for j in range(4):
        for c in range(width // lanes):
            mslots[j, 0:quarter, c * lanes:(c + 1) * lanes] = flat[
                c, pl.ds(j, quarter, stride=4), :
            ].astype(jnp.bfloat16)
        for d in range(n - 1, 0, -1):
            copy_m(j, d).start()

    load_merge.wait()
    acc = None
    for j in range(4):
        for d in range(1, n):
            copy_m(j, d).wait_recv()
        part = jnp.dot(
            mslots[j], wmerge[j * width:(j + 1) * width, :], preferred_element_type=jnp.float32
        )
        acc = part if acc is None else acc + part
    obuf[...] = acc.astype(jnp.bfloat16)
    for d in range(n - 1, 0, -1):
        copy_o(d).start()
    out_ref[:, pl.ds(pl.multiple_of(me * cols, 128), cols)] = obuf[0:quarter, :]

    for d in range(1, n):
        copy_a(d).wait_send()
        copy_p(d).wait_send()
        for j in range(4):
            copy_m(j, d).wait_send()
    for d in range(1, n):
        copy_o(d).wait_send()
        copy_o(d).wait_recv()


def per_device(tokens, segment_ids, w_qkv, w_out, w_merge, gain_attn, gain_merge):
    n = lax.axis_size("seq")
    rows, width = tokens.shape
    heads = HEADS // n
    quarter = rows // 4
    cols = w_merge.shape[1]
    total = n * rows
    vmem = pl.BlockSpec(memory_space=pltpu.VMEM)
    hbm = pl.BlockSpec(memory_space=pl.ANY)
    bf16 = jnp.bfloat16
    dma = pltpu.SemaphoreType.DMA
    return pl.pallas_call(
        functools.partial(block_kernel, n),
        out_shape=jax.ShapeDtypeStruct((quarter, n * cols), bf16),
        in_specs=[vmem, vmem, hbm, hbm, hbm, vmem, vmem],
        out_specs=vmem,
        scratch_shapes=[
            pltpu.VMEM(w_qkv.shape, bf16),
            pltpu.VMEM(w_out.shape, bf16),
            pltpu.VMEM(w_merge.shape, bf16),
            pltpu.VMEM((n, rows, width), bf16),
            pltpu.VMEM((heads, total, HEAD_DIM), bf16),
            pltpu.VMEM((heads, total, HEAD_DIM), bf16),
            pltpu.VMEM((heads, total, HEAD_DIM), bf16),
            pltpu.VMEM((1, total), jnp.float32),
            pltpu.VMEM((rows, heads * HEAD_DIM), bf16),
            pltpu.VMEM((n, rows, width), bf16),
            pltpu.VMEM((n, rows, width), bf16),
            pltpu.VMEM((rows, width), jnp.float32),
            pltpu.VMEM((width // 128, rows, 128), jnp.float32),
            pltpu.VMEM((4, n * quarter, width), bf16),
            pltpu.VMEM((n * quarter, cols), bf16),
            dma((3,)),
            dma((n,)),
            dma((n,)),
            dma((n,)),
            dma((n,)),
            dma((4, n)),
            dma((4, n)),
            dma((n,)),
            dma((n,)),
        ],
        compiler_params=pltpu.CompilerParams(
            collective_id=0, has_side_effects=True, vmem_limit_bytes=56 * 1024 * 1024
        ),
    )(
        tokens, segment_ids.reshape(n, rows), w_qkv, w_out, w_merge,
        gain_attn.reshape(1, width), gain_merge.reshape(1, width),
    )


def solution(mesh):
    placed = (
        P(("dp", "seq"), None),
        P("dp"),
        P(None, "seq"),
        P("seq", None),
        P(None, "seq"),
        P(),
        P(),
    )
    return jax.shard_map(
        per_device, mesh=mesh, in_specs=placed, out_specs=P(("dp", "seq"), None), check_vma=False
    )
```

```python
import functools

import jax
import jax.numpy as jnp
from jax import lax
from jax.experimental import pallas as pl
from jax.experimental.pallas import tpu as pltpu
from jax.sharding import PartitionSpec as P

HEADS = 16
HEAD_DIM = 80
LOG2E = 1.4426950408889634
MESH = pl.DeviceIdType.MESH


def layer_norm(vector, scale_gain):
    average = jnp.mean(vector, axis=-1, keepdims=True)
    centred = vector - average
    spread_sq = jnp.mean(centred * centred, axis=-1, keepdims=True)
    return centred * lax.rsqrt(spread_sq + 1e-06) * scale_gain


def block_kernel(
    n, tok_ref, ids_ref, wqkv_hbm, wout_hbm, wmerge_hbm, ga_ref, gm_ref, out_ref,
    wqkv, wout, wmerge, nslots, qs, ks, vs, key_ids, bias, att, psend, pslots, own, flat, mslots, obuf,
    local_sem, a_send, a_recv, p_send, p_recv, m_send, m_recv, o_send, o_recv,
):
    me = lax.axis_index("seq")
    dp = lax.axis_index("dp")
    rows = tok_ref.shape[0]
    width = tok_ref.shape[1]
    heads = qs.shape[0]
    bits = n.bit_length() - 1
    quarter = rows // 4
    cols = wmerge_hbm.shape[1]

    def peer(d):
        total = 0
        for b in range(bits):
            total = total + (((me // (1 << b)) + (d // (1 << b))) % 2) * (1 << b)
        return total

    def remote(src, dst, send, recv, d):
        return pltpu.make_async_remote_copy(
            src_ref=src, dst_ref=dst, send_sem=send, recv_sem=recv,
            device_id=(dp, peer(d)), device_id_type=MESH,
        )

    def copy_a(d):
        return remote(
            nslots.at[pl.ds(0, rows)], nslots.at[pl.ds(d * rows, rows)], a_send.at[d], a_recv.at[d], d,
        )

    def copy_p(d):
        return remote(psend.at[d], pslots.at[d], p_send.at[d], p_recv.at[d], d)

    def copy_m(j, d):
        return remote(
            mslots.at[j, pl.ds(0, quarter)],
            mslots.at[j, pl.ds(d * quarter, quarter)],
            m_send.at[j, d], m_recv.at[j, d], d,
        )

    def copy_o(d):
        return remote(
            obuf.at[pl.ds(d * quarter, quarter)],
            out_ref.at[:, pl.ds(pl.multiple_of(me * cols, 128), cols)],
            o_send.at[d], o_recv.at[d], d,
        )

    barrier = pltpu.get_barrier_semaphore()
    for d in range(1, n):
        pl.semaphore_signal(barrier, inc=1, device_id=(dp, peer(d)), device_id_type=MESH)
    load_qkv = pltpu.make_async_copy(wqkv_hbm, wqkv, local_sem.at[0])
    load_out = pltpu.make_async_copy(wout_hbm, wout, local_sem.at[1])
    load_merge = pltpu.make_async_copy(wmerge_hbm, wmerge, local_sem.at[2])
    load_qkv.start()
    load_out.start()
    load_merge.start()

    nslots[0:rows, :] = layer_norm(tok_ref[...].astype(jnp.float32), ga_ref[...].reshape(1, width)).astype(jnp.bfloat16)
    pl.semaphore_wait(barrier, n - 1)
    for d in range(n - 1, 0, -1):
        copy_a(d).start()

    for d in range(n):
        id_row = ids_ref[pl.ds(peer(d), 1), :].astype(jnp.float32)
        key_ids[d * rows:(d + 1) * rows, :] = jnp.broadcast_to(id_row, (rows, rows)).T

    load_qkv.wait()
    load_out.wait()

    def qkv_step(i, carry):
        for side in range(2):
            d = 2 * i + side

            @pl.when(d > 0)
            def _():
                copy_a(d).wait_recv()

        at = pl.ds(pl.multiple_of(i * 2 * rows, 2 * rows), 2 * rows)
        for h in range(heads):
            for which in range(3):
                base = HEAD_DIM * (3 * h + which)
                prod = lax.dot_general(
                    wqkv[base:base + HEAD_DIM, :], nslots[at, :], (((1,), (1,)), ((), ())),
                    preferred_element_type=jnp.float32,
                )
                if which == 0:
                    qs[h, :, at] = prod.astype(jnp.bfloat16)
                elif which == 1:
                    ks[h, at, :] = prod.T.astype(jnp.bfloat16)
                else:
                    vs[h, :, at] = prod.astype(jnp.bfloat16)
        return carry

    lax.fori_loop(0, n // 2, qkv_step, 0)

    factor = HEAD_DIM ** (-0.5) * LOG2E

    def attend_step(i, carry):
        first = n - 2 - 2 * i
        at = pl.ds(pl.multiple_of(first * rows, 2 * rows), 2 * rows)
        for side in range(2):
            id_row = ids_ref[pl.ds(peer(first + side), 1), :].astype(jnp.float32)
            bias[:, side * rows:(side + 1) * rows] = jnp.where(
                key_ids[...] == id_row, 0.0, -jnp.inf
            )
        for h in range(heads):
            scores = jnp.dot(ks[h], qs[h, :, at], preferred_element_type=jnp.float32)
            scores = scores * factor + bias[...]
            expo = jnp.exp2(scores - jnp.max(scores, axis=0, keepdims=True))
            row_sum = jnp.sum(expo, axis=0, keepdims=True)
            summed = jnp.dot(vs[h], expo.astype(jnp.bfloat16), preferred_element_type=jnp.float32)
            att[h * HEAD_DIM:(h + 1) * HEAD_DIM, :] = summed / row_sum
        part = jnp.dot(
            att[...].T.astype(jnp.bfloat16), wout[...], preferred_element_type=jnp.float32
        )
        for side in range(1, -1, -1):
            d = first + side
            half = part[side * rows:(side + 1) * rows, :]

            @pl.when(d > 0)
            def _():
                psend[d] = half.astype(jnp.bfloat16)
                copy_p(d).start()

            @pl.when(d == 0)
            def _():
                own[...] = half

        return carry

    lax.fori_loop(0, n // 2, attend_step, 0)

    hidden = own[...] + tok_ref[...].astype(jnp.float32)
    for d in range(n - 1, 0, -1):
        copy_p(d).wait_recv()
        hidden = hidden + pslots[d].astype(jnp.float32)
    normed_two = layer_norm(hidden, gm_ref[...].reshape(1, width))
    lanes = flat.shape[2]
    for c in range(width // lanes):
        flat[c] = normed_two[:, c * lanes:(c + 1) * lanes]
    for j in range(4):
        for c in range(width // lanes):
            mslots[j, 0:quarter, c * lanes:(c + 1) * lanes] = flat[
                c, pl.ds(j, quarter, stride=4), :
            ].astype(jnp.bfloat16)
        for d in range(n - 1, 0, -1):
            copy_m(j, d).start()

    load_merge.wait()
    acc = None
    for j in range(4):
        for d in range(1, n):
            copy_m(j, d).wait_recv()
        part = jnp.dot(
            mslots[j], wmerge[j * width:(j + 1) * width, :], preferred_element_type=jnp.float32
        )
        acc = part if acc is None else acc + part
    obuf[...] = acc.astype(jnp.bfloat16)
    for d in range(n - 1, 0, -1):
        copy_o(d).start()
    out_ref[:, pl.ds(pl.multiple_of(me * cols, 128), cols)] = obuf[0:quarter, :]

    for d in range(1, n):
        copy_a(d).wait_send()
        copy_p(d).wait_send()
        for j in range(4):
            copy_m(j, d).wait_send()
    for d in range(1, n):
        copy_o(d).wait_send()
        copy_o(d).wait_recv()


def per_device(tokens, segment_ids, w_qkv, w_out, w_merge, gain_attn, gain_merge):
    n = lax.axis_size("seq")
    rows, width = tokens.shape
    heads = HEADS // n
    quarter = rows // 4
    cols = w_merge.shape[1]
    total = n * rows
    vmem = pl.BlockSpec(memory_space=pltpu.VMEM)
    hbm = pl.BlockSpec(memory_space=pl.ANY)
    bf16 = jnp.bfloat16
    dma = pltpu.SemaphoreType.DMA
    return pl.pallas_call(
        functools.partial(block_kernel, n),
        out_shape=jax.ShapeDtypeStruct((quarter, n * cols), bf16),
        in_specs=[vmem, vmem, hbm, hbm, hbm, vmem, vmem],
        out_specs=vmem,
        scratch_shapes=[
            pltpu.VMEM(w_qkv.shape[::-1], bf16),
            pltpu.VMEM(w_out.shape, bf16),
            pltpu.VMEM(w_merge.shape, bf16),
            pltpu.VMEM((total, width), bf16),
            pltpu.VMEM((heads, HEAD_DIM, total), bf16),
            pltpu.VMEM((heads, total, HEAD_DIM), bf16),
            pltpu.VMEM((heads, HEAD_DIM, total), bf16),
            pltpu.VMEM((total, rows), jnp.float32),
            pltpu.VMEM((total, 2 * rows), jnp.float32),
            pltpu.VMEM((heads * HEAD_DIM, 2 * rows), jnp.float32),
            pltpu.VMEM((n, rows, width), bf16),
            pltpu.VMEM((n, rows, width), bf16),
            pltpu.VMEM((rows, width), jnp.float32),
            pltpu.VMEM((width // 128, rows, 128), jnp.float32),
            pltpu.VMEM((4, n * quarter, width), bf16),
            pltpu.VMEM((n * quarter, cols), bf16),
            dma((3,)),
            dma((n,)),
            dma((n,)),
            dma((n,)),
            dma((n,)),
            dma((4, n)),
            dma((4, n)),
            dma((n,)),
            dma((n,)),
        ],
        compiler_params=pltpu.CompilerParams(
            collective_id=0, has_side_effects=True, vmem_limit_bytes=56 * 1024 * 1024
        ),
    )(
        tokens, segment_ids.reshape(n, rows), w_qkv.T, w_out, w_merge, gain_attn, gain_merge,
    )


def solution(mesh):
    placed = (
        P(("dp", "seq"), None),
        P("dp"),
        P(None, "seq"),
        P("seq", None),
        P(None, "seq"),
        P(),
        P(),
    )
    return jax.shard_map(
        per_device, mesh=mesh, in_specs=placed, out_specs=P(("dp", "seq"), None), check_vma=False
    )
```

```python
import functools

import jax
import jax.numpy as jnp
from jax import lax
from jax.experimental import pallas as pl
from jax.experimental.pallas import tpu as pltpu
from jax.sharding import PartitionSpec as P

HEADS = 16
HEAD_DIM = 80
LOG2E = 1.4426950408889634
MESH = pl.DeviceIdType.MESH


def layer_norm(vector, scale_gain):
    average = jnp.mean(vector, axis=-1, keepdims=True)
    centred = vector - average
    spread_sq = jnp.mean(centred * centred, axis=-1, keepdims=True)
    return centred * lax.rsqrt(spread_sq + 1e-06) * scale_gain


def block_kernel(
    n, tok_ref, ids_ref, wqkv_hbm, wout_hbm, wmerge_hbm, ga_ref, gm_ref, out_ref,
    wqkv, wout, wmerge, nslots, qs, ks, vs, key_ids, bias, att, psend, pslots, own, flat, mslots, obuf,
    local_sem, a_send, a_recv, ha_send, ha_recv, p_send, p_recv, m_send, m_recv, o_send, o_recv,
):
    me = lax.axis_index("seq")
    dp = lax.axis_index("dp")
    rows = tok_ref.shape[0]
    width = tok_ref.shape[1]
    heads = qs.shape[0]
    bits = n.bit_length() - 1
    quarter = rows // 4
    cols = wmerge_hbm.shape[1]

    def peer(d):
        total = 0
        for b in range(bits):
            total = total + (((me // (1 << b)) + (d // (1 << b))) % 2) * (1 << b)
        return total

    def remote(src, dst, send, recv, d):
        return pltpu.make_async_remote_copy(
            src_ref=src, dst_ref=dst, send_sem=send, recv_sem=recv,
            device_id=(dp, peer(d)), device_id_type=MESH,
        )

    def copy_a(d):
        return remote(
            nslots.at[pl.ds(0, rows)], nslots.at[pl.ds(d * rows, rows)], a_send.at[d], a_recv.at[d], d,
        )

    def copy_p(d):
        return remote(psend.at[d], pslots.at[d], p_send.at[d], p_recv.at[d], d)

    def copy_m(j, d):
        return remote(
            mslots.at[j, pl.ds(0, quarter)],
            mslots.at[j, pl.ds(d * quarter, quarter)],
            m_send.at[j, d], m_recv.at[j, d], d,
        )

    def copy_o(d):
        return remote(
            obuf.at[pl.ds(d * quarter, quarter)],
            out_ref.at[:, pl.ds(pl.multiple_of(me * cols, 128), cols)],
            o_send.at[d], o_recv.at[d], d,
        )

    half_rows = rows // 2
    half_width = width // 2

    def hop_a(d, half):
        at = d * rows + half * half_rows
        source = (1 + half) * rows + half * half_rows if d == 3 else half * half_rows
        return remote(
            nslots.at[pl.ds(source, half_rows)], nslots.at[pl.ds(at, half_rows)],
            ha_send.at[d, half], ha_recv.at[d, half], 2 - half if d == 3 else d,
        )

    def hop_p(k):
        return remote(psend.at[k], pslots.at[k], p_send.at[k], p_recv.at[k], (1, 2, 1, 2, 2, 1)[k])

    def hop_m(j, d):
        source = (1 + j // 2) * quarter if d == 3 else 0
        return remote(
            mslots.at[j, pl.ds(source, quarter)], mslots.at[j, pl.ds(d * quarter, quarter)],
            m_send.at[j, d], m_recv.at[j, d], 2 - j // 2 if d == 3 else d,
        )

    barrier = pltpu.get_barrier_semaphore()
    for d in range(1, n):
        pl.semaphore_signal(barrier, inc=1, device_id=(dp, peer(d)), device_id_type=MESH)
    load_qkv = pltpu.make_async_copy(wqkv_hbm, wqkv, local_sem.at[0])
    load_out = pltpu.make_async_copy(wout_hbm, wout, local_sem.at[1])
    load_merge = pltpu.make_async_copy(wmerge_hbm, wmerge, local_sem.at[2])
    load_qkv.start()
    load_out.start()
    load_merge.start()

    nslots[0:rows, :] = layer_norm(tok_ref[...].astype(jnp.float32), ga_ref[...].reshape(1, width)).astype(jnp.bfloat16)
    pl.semaphore_wait(barrier, n - 1)
    if n == 4:
        for half in range(2):
            hop_a(1, half).start()
            hop_a(2, 1 - half).start()
    else:
        for d in range(n - 1, 0, -1):
            copy_a(d).start()

    for d in range(n):
        id_row = ids_ref[pl.ds(peer(d), 1), :].astype(jnp.float32)
        key_ids[d * rows:(d + 1) * rows, :] = jnp.broadcast_to(id_row, (rows, rows)).T

    load_qkv.wait()
    load_out.wait()

    def wait_pair(i):
        for side in range(2):
            d = 2 * i + side

            @pl.when(d > 0)
            def _():
                copy_a(d).wait_recv()

    def qkv_step(i, carry):
        if n != 4:
            wait_pair(i)
        at = pl.ds(pl.multiple_of(i * 2 * rows, 2 * rows), 2 * rows)
        for h in range(heads):
            for which in range(3):
                base = HEAD_DIM * (3 * h + which)
                prod = lax.dot_general(
                    wqkv[base:base + HEAD_DIM, :], nslots[at, :], (((1,), (1,)), ((), ())),
                    preferred_element_type=jnp.float32,
                )
                if which == 0:
                    qs[h, :, at] = prod.astype(jnp.bfloat16)
                elif which == 1:
                    ks[h, at, :] = prod.T.astype(jnp.bfloat16)
                else:
                    vs[h, :, at] = prod.astype(jnp.bfloat16)
        return carry

    if n == 4:
        hop_a(1, 0).wait_recv()
        hop_a(3, 0).start()
        hop_a(2, 1).wait_recv()
        hop_a(3, 1).start()
        hop_a(1, 1).wait_recv()
        qkv_step(0, 0)
        hop_a(2, 0).wait_recv()
        hop_a(3, 0).wait_recv()
        hop_a(3, 1).wait_recv()
        qkv_step(1, 0)
    else:
        lax.fori_loop(0, n // 2, qkv_step, 0)

    factor = HEAD_DIM ** (-0.5) * LOG2E

    def attend(first):
        at = pl.ds(pl.multiple_of(first * rows, 2 * rows), 2 * rows)
        for side in range(2):
            id_row = ids_ref[pl.ds(peer(first + side), 1), :].astype(jnp.float32)
            bias[:, side * rows:(side + 1) * rows] = jnp.where(
                key_ids[...] == id_row, 0.0, -jnp.inf
            )
        for h in range(heads):
            scores = jnp.dot(ks[h], qs[h, :, at], preferred_element_type=jnp.float32)
            scores = scores * factor + bias[...]
            expo = jnp.exp2(scores - jnp.max(scores, axis=0, keepdims=True))
            row_sum = jnp.sum(expo, axis=0, keepdims=True)
            summed = jnp.dot(vs[h], expo.astype(jnp.bfloat16), preferred_element_type=jnp.float32)
            att[h * HEAD_DIM:(h + 1) * HEAD_DIM, :] = summed / row_sum
        return jnp.dot(
            att[...].T.astype(jnp.bfloat16), wout[...], preferred_element_type=jnp.float32
        )

    def attend_step(i, carry):
        first = n - 2 - 2 * i
        part = attend(first)
        for side in range(1, -1, -1):
            d = first + side
            half = part[side * rows:(side + 1) * rows, :]

            @pl.when(d > 0)
            def _():
                psend[d] = half.astype(jnp.bfloat16)
                copy_p(d).start()

            @pl.when(d == 0)
            def _():
                own[...] = half

        return carry

    def send_part(k, value):
        psend[k] = value.astype(jnp.bfloat16)
        hop_p(k).start()

    tok = tok_ref[...].astype(jnp.float32)
    if n == 4:
        part = attend(2)
        send_part(0, part[rows:, :half_width])
        send_part(1, part[rows:, half_width:])
        send_part(3, part[:rows, half_width:])
        own[:, :half_width] = part[:rows, :half_width]
        part = attend(0)
        send_part(2, part[rows:, :half_width])
        hop_p(1).wait_recv()
        send_part(5, part[rows:, half_width:] + pslots[1].astype(jnp.float32))
        hop_p(0).wait_recv()
        send_part(4, own[:, :half_width] + pslots[0].astype(jnp.float32))
        own[...] = part[:rows, :] + tok
        for k in range(2, 6):
            hop_p(k).wait_recv()
        left = pslots[2].astype(jnp.float32) + pslots[4].astype(jnp.float32)
        right = pslots[3].astype(jnp.float32) + pslots[5].astype(jnp.float32)
        hidden = own[...] + jnp.concatenate([left, right], axis=1)
    else:
        lax.fori_loop(0, n // 2, attend_step, 0)
        hidden = own[...] + tok
        for d in range(n - 1, 0, -1):
            copy_p(d).wait_recv()
            hidden = hidden + pslots[d].astype(jnp.float32)
    normed_two = layer_norm(hidden, gm_ref[...].reshape(1, width))
    lanes = flat.shape[2]
    for c in range(width // lanes):
        flat[c] = normed_two[:, c * lanes:(c + 1) * lanes]
    for j in (0, 2, 1, 3):
        for c in range(width // lanes):
            mslots[j, 0:quarter, c * lanes:(c + 1) * lanes] = flat[
                c, pl.ds(j, quarter, stride=4), :
            ].astype(jnp.bfloat16)
        if n != 4:
            for d in range(n - 1, 0, -1):
                copy_m(j, d).start()
    if n == 4:
        for j in range(4):
            hop_m(j, 1).start()
            hop_m((j + 2) % 4, 2).start()
        for j in range(2):
            hop_m(j, 1).wait_recv()
            hop_m(j, 3).start()
            hop_m(j + 2, 2).wait_recv()
            hop_m(j + 2, 3).start()

    load_merge.wait()
    acc = None
    for j in (0, 2, 1, 3):
        if n == 4:
            hop_m(j, 2 - j // 2).wait_recv()
            hop_m(j, 3).wait_recv()
        else:
            for d in range(1, n):
                copy_m(j, d).wait_recv()
        part = jnp.dot(
            mslots[j], wmerge[j * width:(j + 1) * width, :], preferred_element_type=jnp.float32
        )
        acc = part if acc is None else acc + part
    obuf[...] = acc.astype(jnp.bfloat16)
    for d in range(n - 1, 0, -1):
        copy_o(d).start()
    out_ref[:, pl.ds(pl.multiple_of(me * cols, 128), cols)] = obuf[0:quarter, :]

    if n == 4:
        for k in range(6):
            hop_p(k).wait_send()
        for d in range(1, n):
            for half in range(2):
                hop_a(d, half).wait_send()
            for j in range(4):
                hop_m(j, d).wait_send()
    else:
        for d in range(1, n):
            copy_a(d).wait_send()
            copy_p(d).wait_send()
            for j in range(4):
                copy_m(j, d).wait_send()
    for d in range(1, n):
        copy_o(d).wait_send()
        copy_o(d).wait_recv()


def per_device(tokens, segment_ids, w_qkv, w_out, w_merge, gain_attn, gain_merge):
    n = lax.axis_size("seq")
    rows, width = tokens.shape
    heads = HEADS // n
    quarter = rows // 4
    cols = w_merge.shape[1]
    total = n * rows
    exchange = (6, rows, width // 2) if n == 4 else (n, rows, width)
    vmem = pl.BlockSpec(memory_space=pltpu.VMEM)
    hbm = pl.BlockSpec(memory_space=pl.ANY)
    bf16 = jnp.bfloat16
    dma = pltpu.SemaphoreType.DMA
    return pl.pallas_call(
        functools.partial(block_kernel, n),
        out_shape=jax.ShapeDtypeStruct((quarter, n * cols), bf16),
        in_specs=[vmem, vmem, hbm, hbm, hbm, vmem, vmem],
        out_specs=vmem,
        scratch_shapes=[
            pltpu.VMEM(w_qkv.shape[::-1], bf16),
            pltpu.VMEM(w_out.shape, bf16),
            pltpu.VMEM(w_merge.shape, bf16),
            pltpu.VMEM((total, width), bf16),
            pltpu.VMEM((heads, HEAD_DIM, total), bf16),
            pltpu.VMEM((heads, total, HEAD_DIM), bf16),
            pltpu.VMEM((heads, HEAD_DIM, total), bf16),
            pltpu.VMEM((total, rows), jnp.float32),
            pltpu.VMEM((total, 2 * rows), jnp.float32),
            pltpu.VMEM((heads * HEAD_DIM, 2 * rows), jnp.float32),
            pltpu.VMEM(exchange, bf16),
            pltpu.VMEM(exchange, bf16),
            pltpu.VMEM((rows, width), jnp.float32),
            pltpu.VMEM((width // 128, rows, 128), jnp.float32),
            pltpu.VMEM((4, n * quarter, width), bf16),
            pltpu.VMEM((n * quarter, cols), bf16),
            dma((3,)),
            dma((n,)),
            dma((n,)),
            dma((n, 2)),
            dma((n, 2)),
            dma(exchange[:1]),
            dma(exchange[:1]),
            dma((4, n)),
            dma((4, n)),
            dma((n,)),
            dma((n,)),
        ],
        compiler_params=pltpu.CompilerParams(
            collective_id=0, has_side_effects=True, vmem_limit_bytes=56 * 1024 * 1024
        ),
    )(
        tokens, segment_ids.reshape(n, rows), w_qkv.T, w_out, w_merge, gain_attn, gain_merge,
    )


def solution(mesh):
    placed = (
        P(("dp", "seq"), None),
        P("dp"),
        P(None, "seq"),
        P("seq", None),
        P(None, "seq"),
        P(),
        P(),
    )
    return jax.shard_map(
        per_device, mesh=mesh, in_specs=placed, out_specs=P(("dp", "seq"), None), check_vma=False
    )
```

```python
import functools

import jax
import jax.numpy as jnp
from jax import lax
from jax.experimental import pallas as pl
from jax.experimental.pallas import tpu as pltpu
from jax.sharding import PartitionSpec as P

HEADS = 16
HEAD_DIM = 80
LOG2E = 1.4426950408889634
MESH = pl.DeviceIdType.MESH


def layer_norm(vector, scale_gain):
    average = jnp.mean(vector, axis=-1, keepdims=True)
    centred = vector - average
    spread_sq = jnp.mean(centred * centred, axis=-1, keepdims=True)
    return centred * lax.rsqrt(spread_sq + 1e-06) * scale_gain


def block_kernel(
    n, tok_ref, ids_ref, wqkv_hbm, wout_hbm, wmerge_hbm, ga_ref, gm_ref, out_ref,
    wqkv, wout, wmerge, nslots, qs, ks, vs, key_ids, bias, att, psend, pslots, own, flat, mslots, obuf,
    local_sem, a_send, a_recv, ha_send, ha_recv, p_send, p_recv, m_send, m_recv, o_send, o_recv,
):
    me = lax.axis_index("seq")
    dp = lax.axis_index("dp")
    rows = tok_ref.shape[0]
    width = tok_ref.shape[1]
    heads = qs.shape[0]
    bits = n.bit_length() - 1
    quarter = rows // 4
    cols = wmerge_hbm.shape[1]

    def peer(d):
        total = 0
        for b in range(bits):
            total = total + (((me // (1 << b)) + (d // (1 << b))) % 2) * (1 << b)
        return total

    def remote(src, dst, send, recv, d):
        return pltpu.make_async_remote_copy(
            src_ref=src, dst_ref=dst, send_sem=send, recv_sem=recv,
            device_id=(dp, peer(d)), device_id_type=MESH,
        )

    def copy_a(d):
        return remote(
            nslots.at[pl.ds(0, rows)], nslots.at[pl.ds(d * rows, rows)], a_send.at[d], a_recv.at[d], d,
        )

    def copy_p(d):
        return remote(psend.at[d], pslots.at[d], p_send.at[d, 0], p_recv.at[d, 0], d)

    def copy_m(j, d):
        return remote(
            mslots.at[j, pl.ds(0, quarter)],
            mslots.at[j, pl.ds(d * quarter, quarter)],
            m_send.at[j, d], m_recv.at[j, d], d,
        )

    def copy_o(d):
        return remote(
            obuf.at[pl.ds(d * quarter, quarter)],
            out_ref.at[:, pl.ds(pl.multiple_of(me * cols, 128), cols)],
            o_send.at[0, d], o_recv.at[0, d], d,
        )

    half_rows = rows // 2
    half_width = width // 2

    def hop_a(d, half):
        at = d * rows + half * half_rows
        source = (1 + half) * rows + half * half_rows if d == 3 else half * half_rows
        return remote(
            nslots.at[pl.ds(source, half_rows)], nslots.at[pl.ds(at, half_rows)],
            ha_send.at[d, half], ha_recv.at[d, half], 2 - half if d == 3 else d,
        )

    def hop_p(k, r):
        at = pl.ds(r * half_rows, half_rows)
        return remote(
            psend.at[k, at], pslots.at[k, at], p_send.at[k, r], p_recv.at[k, r],
            (1, 2, 1, 2, 2, 1)[k],
        )

    eighth = quarter // 2

    def hop_m(r, g, d):
        source = (1 + g) * quarter + r * eighth if d == 3 else r * eighth
        pair = pl.ds(2 * g, 2)
        return remote(
            mslots.at[pair, pl.ds(source, eighth)],
            mslots.at[pair, pl.ds(d * quarter + r * eighth, eighth)],
            m_send.at[2 * r + g, d], m_recv.at[2 * r + g, d], 2 - g if d == 3 else d,
        )

    def hop_o(r, d):
        return remote(
            obuf.at[pl.ds((r * n + d) * eighth, eighth)],
            out_ref.at[pl.ds(r * eighth, eighth), pl.ds(pl.multiple_of(me * cols, 128), cols)],
            o_send.at[r, d], o_recv.at[r, d], d,
        )

    barrier = pltpu.get_barrier_semaphore()
    for d in range(1, n):
        pl.semaphore_signal(barrier, inc=1, device_id=(dp, peer(d)), device_id_type=MESH)
    load_qkv = pltpu.make_async_copy(wqkv_hbm, wqkv, local_sem.at[0])
    load_out = pltpu.make_async_copy(wout_hbm, wout, local_sem.at[1])
    load_merge = pltpu.make_async_copy(wmerge_hbm, wmerge, local_sem.at[2])
    load_qkv.start()
    load_out.start()
    load_merge.start()

    nslots[0:rows, :] = layer_norm(tok_ref[...].astype(jnp.float32), ga_ref[...].reshape(1, width)).astype(jnp.bfloat16)
    pl.semaphore_wait(barrier, n - 1)
    if n == 4:
        for half in range(2):
            hop_a(1, half).start()
            hop_a(2, 1 - half).start()
    else:
        for d in range(n - 1, 0, -1):
            copy_a(d).start()

    for d in range(n):
        id_row = ids_ref[pl.ds(peer(d), 1), :].astype(jnp.float32)
        key_ids[d * rows:(d + 1) * rows, :] = jnp.broadcast_to(id_row, (rows, rows)).T

    load_qkv.wait()
    load_out.wait()

    def wait_pair(i):
        for side in range(2):
            d = 2 * i + side

            @pl.when(d > 0)
            def _():
                copy_a(d).wait_recv()

    def qkv_step(i, carry):
        if n != 4:
            wait_pair(i)
        at = pl.ds(pl.multiple_of(i * 2 * rows, 2 * rows), 2 * rows)
        for h in range(heads):
            for which in range(3):
                base = HEAD_DIM * (3 * h + which)
                prod = lax.dot_general(
                    wqkv[base:base + HEAD_DIM, :], nslots[at, :], (((1,), (1,)), ((), ())),
                    preferred_element_type=jnp.float32,
                )
                if which == 0:
                    qs[h, :, at] = prod.astype(jnp.bfloat16)
                elif which == 1:
                    ks[h, at, :] = prod.T.astype(jnp.bfloat16)
                else:
                    vs[h, :, at] = prod.astype(jnp.bfloat16)
        return carry

    if n == 4:
        hop_a(1, 0).wait_recv()
        hop_a(3, 0).start()
        hop_a(2, 1).wait_recv()
        hop_a(3, 1).start()
        hop_a(1, 1).wait_recv()
        qkv_step(0, 0)
        hop_a(2, 0).wait_recv()
        hop_a(3, 0).wait_recv()
        hop_a(3, 1).wait_recv()
        qkv_step(1, 0)
    else:
        lax.fori_loop(0, n // 2, qkv_step, 0)

    factor = HEAD_DIM ** (-0.5) * LOG2E

    def attend(first):
        at = pl.ds(pl.multiple_of(first * rows, 2 * rows), 2 * rows)
        for side in range(2):
            id_row = ids_ref[pl.ds(peer(first + side), 1), :].astype(jnp.float32)
            bias[:, side * rows:(side + 1) * rows] = jnp.where(
                key_ids[...] == id_row, 0.0, -jnp.inf
            )
        for h in range(heads):
            scores = jnp.dot(ks[h], qs[h, :, at], preferred_element_type=jnp.float32)
            scores = scores * factor + bias[...]
            expo = jnp.exp2(scores - jnp.max(scores, axis=0, keepdims=True))
            row_sum = jnp.sum(expo, axis=0, keepdims=True)
            summed = jnp.dot(vs[h], expo.astype(jnp.bfloat16), preferred_element_type=jnp.float32)
            att[h * HEAD_DIM:(h + 1) * HEAD_DIM, :] = summed / row_sum
        return jnp.dot(
            att[...].T.astype(jnp.bfloat16), wout[...], preferred_element_type=jnp.float32
        )

    def attend_step(i, carry):
        first = n - 2 - 2 * i
        part = attend(first)
        for side in range(1, -1, -1):
            d = first + side
            half = part[side * rows:(side + 1) * rows, :]

            @pl.when(d > 0)
            def _():
                psend[d] = half.astype(jnp.bfloat16)
                copy_p(d).start()

            @pl.when(d == 0)
            def _():
                own[...] = half

        return carry

    def send_part(k, r, value):
        psend[k, r * half_rows:(r + 1) * half_rows, :] = value.astype(jnp.bfloat16)
        hop_p(k, r).start()

    def came(k, r):
        return pslots[k, r * half_rows:(r + 1) * half_rows, :].astype(jnp.float32)

    lanes = flat.shape[2]

    def put_merged(first, count, value):
        for c in range(width // lanes):
            flat[c, first:first + count, :] = value[:, c * lanes:(c + 1) * lanes]
        for j in range(4):
            for c in range(width // lanes):
                mslots[j, first // 4:(first + count) // 4, c * lanes:(c + 1) * lanes] = flat[
                    c, pl.ds(first + j, count // 4, stride=4), :
                ].astype(jnp.bfloat16)

    tok = tok_ref[...].astype(jnp.float32)
    mine = pl.ds(pl.multiple_of(me * cols, 128), cols)
    if n == 4:
        halves = [(r, slice(r * half_rows, (r + 1) * half_rows)) for r in range(2)]
        part = attend(2)
        near, far = part[:rows, :], part[rows:, :]
        for r, at in halves:
            send_part(0, r, far[at, :half_width])
            send_part(1, r, far[at, half_width:])
        for r, at in halves:
            send_part(3, r, near[at, half_width:])
        own[:, :half_width] = near[:, :half_width]
        part = attend(0)
        near, far = part[:rows, :], part[rows:, :]
        for r, at in halves:
            send_part(2, r, far[at, :half_width])
            hop_p(1, r).wait_recv()
            send_part(5, r, far[at, half_width:] + came(1, r))
            hop_p(0, r).wait_recv()
            send_part(4, r, own[at, :half_width] + came(0, r))
        own[...] = near + tok
        for r, at in halves:
            for k in range(2, 6):
                hop_p(k, r).wait_recv()
            summed = jnp.concatenate(
                [came(2, r) + came(4, r), came(3, r) + came(5, r)], axis=1
            )
            hidden = own[at, :] + summed
            put_merged(
                r * half_rows, half_rows, layer_norm(hidden, gm_ref[...].reshape(1, width))
            )
            for g in range(2):
                hop_m(r, g, 1).start()
                hop_m(r, 1 - g, 2).start()
        for r in range(2):
            hop_m(r, 0, 1).wait_recv()
            hop_m(r, 0, 3).start()
            hop_m(r, 1, 2).wait_recv()
            hop_m(r, 1, 3).start()
        load_merge.wait()
        for r in range(2):
            acc = None
            for j in range(4):
                if j % 2 == 0:
                    hop_m(r, j // 2, 2 - j // 2).wait_recv()
                    hop_m(r, j // 2, 3).wait_recv()
                block = jnp.concatenate(
                    [
                        mslots[j, d * quarter + r * eighth:d * quarter + (r + 1) * eighth, :]
                        for d in range(n)
                    ],
                    axis=0,
                )
                part = jnp.dot(
                    block, wmerge[j * width:(j + 1) * width, :],
                    preferred_element_type=jnp.float32,
                )
                acc = part if acc is None else acc + part
            obuf[r * n * eighth:(r + 1) * n * eighth, :] = acc.astype(jnp.bfloat16)
            for d in range(n - 1, 0, -1):
                hop_o(r, d).start()
            out_ref[r * eighth:(r + 1) * eighth, mine] = obuf[
                r * n * eighth:r * n * eighth + eighth, :
            ]
        for r in range(2):
            for k in range(6):
                hop_p(k, r).wait_send()
            for d in range(1, n):
                hop_a(d, r).wait_send()
                for g in range(2):
                    hop_m(r, g, d).wait_send()
                hop_o(r, d).wait_send()
                hop_o(r, d).wait_recv()
    else:
        lax.fori_loop(0, n // 2, attend_step, 0)
        hidden = own[...] + tok
        for d in range(n - 1, 0, -1):
            copy_p(d).wait_recv()
            hidden = hidden + pslots[d].astype(jnp.float32)
        put_merged(0, rows, layer_norm(hidden, gm_ref[...].reshape(1, width)))
        for j in range(4):
            for d in range(n - 1, 0, -1):
                copy_m(j, d).start()
        load_merge.wait()
        acc = None
        for j in range(4):
            for d in range(1, n):
                copy_m(j, d).wait_recv()
            part = jnp.dot(
                mslots[j], wmerge[j * width:(j + 1) * width, :],
                preferred_element_type=jnp.float32,
            )
            acc = part if acc is None else acc + part
        obuf[...] = acc.astype(jnp.bfloat16)
        for d in range(n - 1, 0, -1):
            copy_o(d).start()
        out_ref[:, mine] = obuf[0:quarter, :]
        for d in range(1, n):
            copy_a(d).wait_send()
            copy_p(d).wait_send()
            for j in range(4):
                copy_m(j, d).wait_send()
            copy_o(d).wait_send()
            copy_o(d).wait_recv()


def per_device(tokens, segment_ids, w_qkv, w_out, w_merge, gain_attn, gain_merge):
    n = lax.axis_size("seq")
    rows, width = tokens.shape
    heads = HEADS // n
    quarter = rows // 4
    cols = w_merge.shape[1]
    total = n * rows
    exchange = (6, rows, width // 2) if n == 4 else (n, rows, width)
    vmem = pl.BlockSpec(memory_space=pltpu.VMEM)
    hbm = pl.BlockSpec(memory_space=pl.ANY)
    bf16 = jnp.bfloat16
    dma = pltpu.SemaphoreType.DMA
    return pl.pallas_call(
        functools.partial(block_kernel, n),
        out_shape=jax.ShapeDtypeStruct((quarter, n * cols), bf16),
        in_specs=[vmem, vmem, hbm, hbm, hbm, vmem, vmem],
        out_specs=vmem,
        scratch_shapes=[
            pltpu.VMEM(w_qkv.shape[::-1], bf16),
            pltpu.VMEM(w_out.shape, bf16),
            pltpu.VMEM(w_merge.shape, bf16),
            pltpu.VMEM((total, width), bf16),
            pltpu.VMEM((heads, HEAD_DIM, total), bf16),
            pltpu.VMEM((heads, total, HEAD_DIM), bf16),
            pltpu.VMEM((heads, HEAD_DIM, total), bf16),
            pltpu.VMEM((total, rows), jnp.float32),
            pltpu.VMEM((total, 2 * rows), jnp.float32),
            pltpu.VMEM((heads * HEAD_DIM, 2 * rows), jnp.float32),
            pltpu.VMEM(exchange, bf16),
            pltpu.VMEM(exchange, bf16),
            pltpu.VMEM((rows, width), jnp.float32),
            pltpu.VMEM((width // 128, rows, 128), jnp.float32),
            pltpu.VMEM((4, n * quarter, width), bf16),
            pltpu.VMEM((n * quarter, cols), bf16),
            dma((3,)),
            dma((n,)),
            dma((n,)),
            dma((n, 2)),
            dma((n, 2)),
            dma((exchange[0], 2)),
            dma((exchange[0], 2)),
            dma((4, n)),
            dma((4, n)),
            dma((2, n)),
            dma((2, n)),
        ],
        compiler_params=pltpu.CompilerParams(
            collective_id=0, has_side_effects=True, vmem_limit_bytes=56 * 1024 * 1024
        ),
    )(
        tokens, segment_ids.reshape(n, rows), w_qkv.T, w_out, w_merge, gain_attn, gain_merge,
    )


def solution(mesh):
    placed = (
        P(("dp", "seq"), None),
        P("dp"),
        P(None, "seq"),
        P("seq", None),
        P(None, "seq"),
        P(),
        P(),
    )
    return jax.shard_map(
        per_device, mesh=mesh, in_specs=placed, out_specs=P(("dp", "seq"), None), check_vma=False
    )
```

```python
import functools

import jax
import jax.numpy as jnp
from jax import lax
from jax.experimental import pallas as pl
from jax.experimental.pallas import tpu as pltpu
from jax.sharding import PartitionSpec as P

HEADS = 16
HEAD_DIM = 80
LOG2E = 1.4426950408889634
MESH = pl.DeviceIdType.MESH


def layer_norm(vector, scale_gain):
    average = jnp.mean(vector, axis=-1, keepdims=True)
    centred = vector - average
    spread_sq = jnp.mean(centred * centred, axis=-1, keepdims=True)
    return centred * lax.rsqrt(spread_sq + 1e-06) * scale_gain


def block_kernel(
    n, tok_ref, ids_ref, wqkv_hbm, wout_hbm, wmerge_hbm, ga_ref, gm_ref, out_ref,
    wqkv, wout, wmerge, nslots, qs, ks, vs, key_ids, bias, att, psend, pslots, own, flat, mslots, obuf,
    local_sem, a_send, a_recv, ha_send, ha_recv, p_send, p_recv, m_send, m_recv, o_send, o_recv,
):
    me = lax.axis_index("seq")
    dp = lax.axis_index("dp")
    rows = tok_ref.shape[0]
    width = tok_ref.shape[1]
    heads = qs.shape[0]
    bits = n.bit_length() - 1
    quarter = rows // 4
    cols = wmerge_hbm.shape[1]

    def peer(d):
        total = 0
        for b in range(bits):
            total = total + (((me // (1 << b)) + (d // (1 << b))) % 2) * (1 << b)
        return total

    def remote(src, dst, send, recv, d):
        return pltpu.make_async_remote_copy(
            src_ref=src, dst_ref=dst, send_sem=send, recv_sem=recv,
            device_id=(dp, peer(d)), device_id_type=MESH,
        )

    def copy_a(d):
        return remote(
            nslots.at[pl.ds(0, rows)], nslots.at[pl.ds(d * rows, rows)], a_send.at[d], a_recv.at[d], d,
        )

    def copy_p(d):
        return remote(psend.at[d], pslots.at[d], p_send.at[d], p_recv.at[d], d)

    def copy_m(j, d):
        return remote(
            mslots.at[j, pl.ds(0, quarter)],
            mslots.at[j, pl.ds(d * quarter, quarter)],
            m_send.at[j, d], m_recv.at[j, d], d,
        )

    def copy_o(d):
        return remote(
            obuf.at[pl.ds(d * quarter, quarter)],
            out_ref.at[:, pl.ds(pl.multiple_of(me * cols, 128), cols)],
            o_send.at[d], o_recv.at[d], d,
        )

    half_rows = rows // 2
    half_width = width // 2

    def hop_a(d, half):
        at = d * rows + half * half_rows
        source = (1 + half) * rows + half * half_rows if d == 3 else half * half_rows
        return remote(
            nslots.at[pl.ds(source, half_rows)], nslots.at[pl.ds(at, half_rows)],
            ha_send.at[d, half], ha_recv.at[d, half], 2 - half if d == 3 else d,
        )

    def hop_p(k):
        return remote(psend.at[k], pslots.at[k], p_send.at[k], p_recv.at[k], (1, 2, 1, 2, 2, 1)[k])

    def hop_m(j, d):
        source = (1 + j // 2) * quarter if d == 3 else 0
        return remote(
            mslots.at[j, pl.ds(source, quarter)], mslots.at[j, pl.ds(d * quarter, quarter)],
            m_send.at[j, d], m_recv.at[j, d], 2 - j // 2 if d == 3 else d,
        )

    barrier = pltpu.get_barrier_semaphore()
    for d in range(1, n):
        pl.semaphore_signal(barrier, inc=1, device_id=(dp, peer(d)), device_id_type=MESH)
    load_qkv = pltpu.make_async_copy(wqkv_hbm, wqkv, local_sem.at[0])
    load_out = pltpu.make_async_copy(wout_hbm, wout, local_sem.at[1])
    load_merge = pltpu.make_async_copy(wmerge_hbm, wmerge, local_sem.at[2])
    load_qkv.start()
    load_out.start()
    load_merge.start()

    nslots[0:rows, :] = layer_norm(tok_ref[...].astype(jnp.float32), ga_ref[...].reshape(1, width)).astype(jnp.bfloat16)
    pl.semaphore_wait(barrier, n - 1)
    if n == 4:
        for half in range(2):
            hop_a(1, half).start()
            hop_a(2, 1 - half).start()
    else:
        for d in range(n - 1, 0, -1):
            copy_a(d).start()

    for d in range(n):
        id_row = ids_ref[pl.ds(peer(d), 1), :].astype(jnp.float32)
        key_ids[d * rows:(d + 1) * rows, :] = jnp.broadcast_to(id_row, (rows, rows)).T

    load_qkv.wait()
    load_out.wait()

    def wait_pair(i):
        for side in range(2):
            d = 2 * i + side

            @pl.when(d > 0)
            def _():
                copy_a(d).wait_recv()

    def qkv_step(i, carry):
        if n != 4:
            wait_pair(i)
        at = pl.ds(pl.multiple_of(i * 2 * rows, 2 * rows), 2 * rows)
        prod = lax.dot_general(
            wqkv[...], nslots[at, :], (((1,), (1,)), ((), ())),
            preferred_element_type=jnp.float32,
        )
        for h in range(heads):
            base = 3 * HEAD_DIM * h
            query = prod[base:base + HEAD_DIM, :]
            key = prod[base + HEAD_DIM:base + 2 * HEAD_DIM, :]
            value = prod[base + 2 * HEAD_DIM:base + 3 * HEAD_DIM, :]
            qs[h, :, at] = query.astype(jnp.bfloat16)
            ks[h, at, :] = key.T.astype(jnp.bfloat16)
            vs[h, :, at] = value.astype(jnp.bfloat16)
        return carry

    if n == 4:
        hop_a(1, 0).wait_recv()
        hop_a(3, 0).start()
        hop_a(2, 1).wait_recv()
        hop_a(3, 1).start()
        hop_a(1, 1).wait_recv()
        qkv_step(0, 0)
        hop_a(2, 0).wait_recv()
        hop_a(3, 0).wait_recv()
        hop_a(3, 1).wait_recv()
        qkv_step(1, 0)
    else:
        lax.fori_loop(0, n // 2, qkv_step, 0)

    factor = HEAD_DIM ** (-0.5) * LOG2E

    def attend(first):
        at = pl.ds(pl.multiple_of(first * rows, 2 * rows), 2 * rows)
        for side in range(2):
            id_row = ids_ref[pl.ds(peer(first + side), 1), :].astype(jnp.float32)
            bias[:, side * rows:(side + 1) * rows] = jnp.where(
                key_ids[...] == id_row, 0.0, -jnp.inf
            )
        for h in range(heads):
            scores = jnp.dot(ks[h], qs[h, :, at], preferred_element_type=jnp.float32)
            scores = scores * factor + bias[...]
            expo = jnp.exp2(scores - jnp.max(scores, axis=0, keepdims=True))
            row_sum = jnp.sum(expo, axis=0, keepdims=True)
            summed = jnp.dot(vs[h], expo.astype(jnp.bfloat16), preferred_element_type=jnp.float32)
            att[h * HEAD_DIM:(h + 1) * HEAD_DIM, :] = summed / row_sum
        return jnp.dot(
            att[...].T.astype(jnp.bfloat16), wout[...], preferred_element_type=jnp.float32
        )

    def attend_step(i, carry):
        first = n - 2 - 2 * i
        part = attend(first)
        for side in range(1, -1, -1):
            d = first + side
            half = part[side * rows:(side + 1) * rows, :]

            @pl.when(d > 0)
            def _():
                psend[d] = half.astype(jnp.bfloat16)
                copy_p(d).start()

            @pl.when(d == 0)
            def _():
                own[...] = half

        return carry

    def send_part(k, value):
        psend[k] = value.astype(jnp.bfloat16)
        hop_p(k).start()

    tok = tok_ref[...].astype(jnp.float32)
    if n == 4:
        part = attend(2)
        send_part(0, part[rows:, :half_width])
        send_part(1, part[rows:, half_width:])
        send_part(3, part[:rows, half_width:])
        own[:, :half_width] = part[:rows, :half_width]
        part = attend(0)
        send_part(2, part[rows:, :half_width])
        hop_p(1).wait_recv()
        send_part(5, part[rows:, half_width:] + pslots[1].astype(jnp.float32))
        hop_p(0).wait_recv()
        send_part(4, own[:, :half_width] + pslots[0].astype(jnp.float32))
        own[...] = part[:rows, :] + tok
        for k in range(2, 6):
            hop_p(k).wait_recv()
        left = pslots[2].astype(jnp.float32) + pslots[4].astype(jnp.float32)
        right = pslots[3].astype(jnp.float32) + pslots[5].astype(jnp.float32)
        hidden = own[...] + jnp.concatenate([left, right], axis=1)
    else:
        lax.fori_loop(0, n // 2, attend_step, 0)
        hidden = own[...] + tok
        for d in range(n - 1, 0, -1):
            copy_p(d).wait_recv()
            hidden = hidden + pslots[d].astype(jnp.float32)
    normed_two = layer_norm(hidden, gm_ref[...].reshape(1, width))
    lanes = flat.shape[2]
    for c in range(width // lanes):
        flat[c] = normed_two[:, c * lanes:(c + 1) * lanes]
    for j in (0, 2, 1, 3):
        for c in range(width // lanes):
            mslots[j, 0:quarter, c * lanes:(c + 1) * lanes] = flat[
                c, pl.ds(j, quarter, stride=4), :
            ].astype(jnp.bfloat16)
        if n != 4:
            for d in range(n - 1, 0, -1):
                copy_m(j, d).start()
    if n == 4:
        for j in range(4):
            hop_m(j, 1).start()
            hop_m((j + 2) % 4, 2).start()
        for j in range(2):
            hop_m(j, 1).wait_recv()
            hop_m(j, 3).start()
            hop_m(j + 2, 2).wait_recv()
            hop_m(j + 2, 3).start()

    load_merge.wait()
    acc = None
    for j in (0, 2, 1, 3):
        if n == 4:
            hop_m(j, 2 - j // 2).wait_recv()
            hop_m(j, 3).wait_recv()
        else:
            for d in range(1, n):
                copy_m(j, d).wait_recv()
        part = jnp.dot(
            mslots[j], wmerge[j * width:(j + 1) * width, :], preferred_element_type=jnp.float32
        )
        acc = part if acc is None else acc + part
    obuf[...] = acc.astype(jnp.bfloat16)
    for d in range(n - 1, 0, -1):
        copy_o(d).start()
    out_ref[:, pl.ds(pl.multiple_of(me * cols, 128), cols)] = obuf[0:quarter, :]

    if n == 4:
        for k in range(6):
            hop_p(k).wait_send()
        for d in range(1, n):
            for half in range(2):
                hop_a(d, half).wait_send()
            for j in range(4):
                hop_m(j, d).wait_send()
    else:
        for d in range(1, n):
            copy_a(d).wait_send()
            copy_p(d).wait_send()
            for j in range(4):
                copy_m(j, d).wait_send()
    for d in range(1, n):
        copy_o(d).wait_send()
        copy_o(d).wait_recv()


def per_device(tokens, segment_ids, w_qkv, w_out, w_merge, gain_attn, gain_merge):
    n = lax.axis_size("seq")
    rows, width = tokens.shape
    heads = HEADS // n
    quarter = rows // 4
    cols = w_merge.shape[1]
    total = n * rows
    exchange = (6, rows, width // 2) if n == 4 else (n, rows, width)
    vmem = pl.BlockSpec(memory_space=pltpu.VMEM)
    hbm = pl.BlockSpec(memory_space=pl.ANY)
    bf16 = jnp.bfloat16
    dma = pltpu.SemaphoreType.DMA
    return pl.pallas_call(
        functools.partial(block_kernel, n),
        out_shape=jax.ShapeDtypeStruct((quarter, n * cols), bf16),
        in_specs=[vmem, vmem, hbm, hbm, hbm, vmem, vmem],
        out_specs=vmem,
        scratch_shapes=[
            pltpu.VMEM(w_qkv.shape[::-1], bf16),
            pltpu.VMEM(w_out.shape, bf16),
            pltpu.VMEM(w_merge.shape, bf16),
            pltpu.VMEM((total, width), bf16),
            pltpu.VMEM((heads, HEAD_DIM, total), bf16),
            pltpu.VMEM((heads, total, HEAD_DIM), bf16),
            pltpu.VMEM((heads, HEAD_DIM, total), bf16),
            pltpu.VMEM((total, rows), jnp.float32),
            pltpu.VMEM((total, 2 * rows), jnp.float32),
            pltpu.VMEM((heads * HEAD_DIM, 2 * rows), jnp.float32),
            pltpu.VMEM(exchange, bf16),
            pltpu.VMEM(exchange, bf16),
            pltpu.VMEM((rows, width), jnp.float32),
            pltpu.VMEM((width // 128, rows, 128), jnp.float32),
            pltpu.VMEM((4, n * quarter, width), bf16),
            pltpu.VMEM((n * quarter, cols), bf16),
            dma((3,)),
            dma((n,)),
            dma((n,)),
            dma((n, 2)),
            dma((n, 2)),
            dma(exchange[:1]),
            dma(exchange[:1]),
            dma((4, n)),
            dma((4, n)),
            dma((n,)),
            dma((n,)),
        ],
        compiler_params=pltpu.CompilerParams(
            collective_id=0, has_side_effects=True, vmem_limit_bytes=56 * 1024 * 1024
        ),
    )(
        tokens, segment_ids.reshape(n, rows), w_qkv.T, w_out, w_merge, gain_attn, gain_merge,
    )


def solution(mesh):
    placed = (
        P(("dp", "seq"), None),
        P("dp"),
        P(None, "seq"),
        P("seq", None),
        P(None, "seq"),
        P(),
        P(),
    )
    return jax.shard_map(
        per_device, mesh=mesh, in_specs=placed, out_specs=P(("dp", "seq"), None), check_vma=False
    )
```
